32 devices in a mesh: ao: 4 (over z), vir: 4 (over y, core), occ: 2 (over x).
Axes of the slice: x: 2, y: 2, z: 4, core: 2. Of those that a mesh axis runs over, the one named last changes fastest.
Arguments:
- pair_list: int32 [10, 2], P('occ'), may hold values from 0 to 3, as said below
- half_ints: bfloat16 [2560, 4, 6144], P('ao', 'occ', 'vir'), may hold values from -6 to 6
- vir_coef: bfloat16 [2560, 2048], P('ao'), may hold values from -0.125 to 0.125
- metric: bfloat16 [6144, 6144], P('vir'), may hold values from -2 to 2, as said below
- occ_energy: float32 [4], replicated, may hold values from -2 to -0.3
- vir_energy: float32 [2048], replicated, may hold values from 0.2 to 3
Outputs:
- density: float32 [2048, 4, 6144], P('vir', 'occ', 'ao')
The draws below stay inside these ranges and needn't reach their ends.
Inputs may be any that keep to these rules, and one draw needn't show every extreme that they name: `pair_list`: each unordered pair of the window's orbitals (an orbital with itself included) appears once, in an order and an orientation (i, j) or (j, i) drawn from the seed. `metric`: symmetric.
All inputs are finite; a program needn't handle non-finite values.
Results may differ from the reference program's by a relative error of at most 0.006.
Values may be sent and summed in bfloat16 or wider, within the bound.
No kernel may reach another device: no remote copies, remote signals or barrier semaphores. Data moves between devices by JAX's collectives and lax.ppermute only.
A program may use at most 192 MiB of HBM per device.

```python
import math
import jax
import jax.numpy as jnp
from jax import lax

NAO = 2560
NVIR = 2048
NAUX = 6144
OCC_WIN = 4
PAIRS = 10


def draw_pair_list(key, part):
    order_key = jax.random.fold_in(key, 29)
    flip_key = jax.random.fold_in(key, 31)
    rows, cols = jnp.triu_indices(OCC_WIN)
    rows = rows.astype(jnp.int32)
    cols = cols.astype(jnp.int32)
    flips = jax.random.randint(flip_key, (PAIRS,), 0, 2).astype(jnp.int32)
    first = jnp.where(flips == 1, cols, rows)
    second = jnp.where(flips == 1, rows, cols)
    table = jnp.stack([first, second], axis=1).astype(jnp.int32)
    order = jax.random.permutation(order_key, PAIRS)
    return table[order]


def draw_metric(key, part):
    noise_key, diag_key = jax.random.split(jax.random.fold_in(key, 17), 2)
    level = NAUX ** (-0.25)
    noise = jax.random.normal(noise_key, (NAUX, NAUX), jnp.float32)
    spread = 0.5 * level / math.sqrt(2.0 * NAUX)
    matrix = (noise + noise.T) * spread
    diag_vals = level * jax.random.uniform(diag_key, (NAUX,), jnp.float32, 0.8, 1.2)
    matrix = matrix + jnp.diag(diag_vals)
    return matrix.astype(jnp.bfloat16)


def block_levels(stream_key, dims, shards, least, top_value):
    factor_of, own = 1.0, jax.random.fold_in(stream_key, 6)
    for axis_at, blocks in shards:
        steps = jnp.exp(jax.random.uniform(jax.random.fold_in(own, axis_at), (blocks,), jnp.float32, least / len(shards), top_value / len(shards)))
        factor_of = factor_of * jnp.repeat(steps, dims[axis_at] // blocks).reshape([-1 if axis == axis_at else 1 for axis in range(len(dims))])
    return factor_of


def centred(key, shape, deviation, most, pieces=(), kind=jnp.bfloat16):
    level = block_levels(key, shape, pieces, -0.22, 0.18) if pieces else 1.0
    array = jax.random.normal(key, shape, jnp.float32) * deviation * level
    return jnp.minimum(jnp.maximum(array, -most), most).astype(kind)


def setup_inputs(seed: int = 0) -> dict:
    key_of = jax.random.split(jax.random.key(seed), 7)
    return {
        "pair_list": draw_pair_list(jax.random.fold_in(key_of[6], 71), 0),
        "half_ints": centred(key_of[1], (NAO, OCC_WIN, NAUX), 1.0, 6.0, ((0, 4), (1, 2), (2, 4))),
        "vir_coef": centred(key_of[2], (NAO, NVIR), NAO ** -0.5, 0.125, ((0, 4),)),
        "metric": draw_metric(jax.random.fold_in(key_of[6], 71), 0),
        "occ_energy": jnp.clip(jax.random.uniform(key_of[4], (OCC_WIN,), jnp.float32, -2.0, -0.3), -2.0, -0.3),
        "vir_energy": jnp.clip(jax.random.uniform(key_of[5], (NVIR,), jnp.float32, 0.2, 3.0), 0.2, 3.0),
    }


def reference(pair_list, half_ints, vir_coef, metric, occ_energy, vir_energy):
    flat_half = half_ints.reshape(NAO, OCC_WIN * NAUX)
    transformed = jnp.dot(vir_coef.T, flat_half, preferred_element_type=jnp.float32).astype(jnp.bfloat16)
    fitted = jnp.dot(transformed.reshape(NVIR * OCC_WIN, NAUX), metric, preferred_element_type=jnp.float32)
    fitted = fitted.astype(jnp.bfloat16).reshape(NVIR, OCC_WIN, NAUX)
    levels = jnp.arange(OCC_WIN, dtype=jnp.int32)

    def one_pair(total, pair):
        first = pair[0]
        second = pair[1]
        left = lax.dynamic_index_in_dim(fitted, first, 1, keepdims=False)
        right = lax.dynamic_index_in_dim(fitted, second, 1, keepdims=False)
        coulomb = jnp.dot(left, right.T, preferred_element_type=jnp.float32)
        occ_sum = occ_energy[first] + occ_energy[second]
        denom = (vir_energy[:, None] + vir_energy[None, :]) - occ_sum
        amplitude = (-coulomb / denom).astype(jnp.bfloat16)
        density = jnp.dot(amplitude, right, preferred_element_type=jnp.float32)
        marks = (levels == first).astype(jnp.float32)
        return total + density[:, None, :] * marks[None, :, None], None

    total, _ = lax.scan(one_pair, jnp.zeros((NVIR, OCC_WIN, NAUX), jnp.float32), pair_list)
    return total
```

```python
import functools

import jax
import jax.numpy as jnp
from jax import lax
from jax.experimental import pallas as pl
from jax.experimental.pallas import tpu as pltpu
from jax.sharding import Mesh, PartitionSpec as P

BF = jnp.bfloat16
F32 = jnp.float32
VMEM = 56 * 1024 * 1024
NT = (((1,), (1,)), ((), ()))


def swap(value, axis):
    return lax.ppermute(value, axis, [(0, 1), (1, 0)])


def tile_of(width):
    return 256 if width % 256 == 0 else width


def cost(flops, nbytes):
    return pl.CostEstimate(flops=int(flops), bytes_accessed=int(nbytes), transcendentals=0)


def call(kernel, prefetch, operands, grid, in_specs, out_specs, out_shape, scratch, estimate, name):
    return pl.pallas_call(
        kernel,
        grid_spec=pltpu.PrefetchScalarGridSpec(
            num_scalar_prefetch=1,
            grid=grid,
            in_specs=in_specs,
            out_specs=out_specs,
            scratch_shapes=scratch,
        ),
        out_shape=out_shape,
        compiler_params=pltpu.CompilerParams(vmem_limit_bytes=VMEM),
        cost_estimate=estimate,
        name=name,
    )(prefetch, *operands)


def fit(pieces, owners, metric, half):
    rows, depth = pieces[0].shape
    block, total = metric.shape
    width = block // 2
    tile = tile_of(width)
    steps = width // tile
    count = len(pieces)

    def kernel(index, *refs):
        held, metric_ref, out = refs[:count], refs[count], refs[count + 1]
        acc = None
        for at in range(count):
            columns = pl.ds(pl.multiple_of(index[1 + at] * depth, 128), depth)
            term = lax.dot_general(
                held[at][...], metric_ref[:, columns], NT, preferred_element_type=F32
            )
            acc = term if acc is None else acc + term
        out[...] = acc.astype(BF)

    return call(
        kernel,
        jnp.concatenate([jnp.reshape(half, (1,)), owners]).astype(jnp.int32),
        (*pieces, metric),
        (steps,),
        [pl.BlockSpec((rows, depth), lambda t, index: (0, 0))] * count
        + [pl.BlockSpec((tile, total), lambda t, index: (index[0] * steps + t, 0))],
        pl.BlockSpec((rows, tile), lambda t, index: (0, t)),
        jax.ShapeDtypeStruct((rows, width), BF),
        [],
        cost(2 * rows * total * width, 2 * (rows * total + width * total + rows * width)),
        "fit",
    )


def coulomb(own, sib, pairs, flips, blocks, a_block, rows, segments):
    orbitals = sorted(own)
    n_virt, width = own[orbitals[0]].shape
    count = blocks.shape[0]
    bw = n_virt // count
    n_orb, n_pairs = len(orbitals), len(pairs)
    half = rows // 2
    n_seg = len(segments)
    mixed = [pair for pair in pairs if pair[0] != pair[1]]

    def kernel(index, *refs):
        left = [refs[at * n_orb : (at + 1) * n_orb] for at in range(2)]
        right = [refs[(2 + at) * n_orb : (3 + at) * n_orb] for at in range(2)]
        outs = refs[4 * n_orb : 4 * n_orb + 2 * n_seg]
        acc = refs[4 * n_orb + 2 * n_seg]
        step = pl.program_id(0)

        def product(first, second):
            total = None
            for side in range(2):
                term = lax.dot_general(
                    left[side][orbitals.index(first)][...],
                    right[side][orbitals.index(second)][...],
                    NT,
                    preferred_element_type=F32,
                )
                total = term if total is None else total + term
            return total.astype(BF)

        for at, (i, j) in enumerate(pairs):
            if i == j:
                acc[at] = product(i, j)
            else:
                flip = index[1 + count + mixed.index((i, j))]

                @pl.when(flip == 0)
                def _(at=at, i=i, j=j):
                    acc[at] = product(i, j)

                @pl.when(flip != 0)
                def _(at=at, i=i, j=j):
                    acc[at] = product(j, i)

        start = 0
        for seg, length in enumerate(segments):

            @pl.when((step >= start) & (step < start + length))
            def _(seg=seg):
                for part in range(2):
                    outs[part * n_seg + seg][0] = acc[:, part * half : (part + 1) * half, :]

            start += length

    starts = [sum(segments[:at]) for at in range(n_seg)]
    out_specs = [
        pl.BlockSpec(
            (1, n_pairs, half, bw),
            lambda t, index, start=start, length=length: (
                jnp.clip(t - start, 0, length - 1),
                0,
                0,
                0,
            ),
        )
        for _ in range(2)
        for start, length in zip(starts, segments)
    ]
    out_shape = [
        jax.ShapeDtypeStruct((length, n_pairs, half, bw), BF)
        for _ in range(2)
        for length in segments
    ]
    arrays = [own[o] for o in orbitals] + [sib[o] for o in orbitals]
    index = jnp.concatenate(
        [jnp.reshape(a_block, (1,)), blocks]
        + [jnp.reshape(flips[pair], (1,)) for pair in mixed]
    ).astype(jnp.int32)
    outs = call(
        kernel,
        index,
        (*arrays, *arrays),
        (count,),
        [pl.BlockSpec((rows, width), lambda t, index: (index[0], 0))] * (2 * n_orb)
        + [pl.BlockSpec((bw, width), lambda t, index: (index[1 + t], 0))] * (2 * n_orb),
        out_specs,
        out_shape,
        [pltpu.VMEM((n_pairs, rows, bw), BF)],
        cost(
            4 * n_pairs * rows * n_virt * width,
            4 * n_orb * n_virt * width + 2 * n_pairs * rows * n_virt,
        ),
        "coulomb",
    )
    return [list(outs[part * n_seg : (part + 1) * n_seg]) for part in range(2)]


def contract(groups, own, sib, flips, blocks, core, n_v):
    n_orb = len(own)
    n_virt, width = own[0].shape
    count = blocks.shape[0]
    bw = n_virt // count
    tile = tile_of(width)
    steps = width // tile
    pairs = [pair for group, _ in groups for pair in group]
    mixed = [pair for pair in pairs if pair[0] != pair[1]]
    pieces = [piece for _, held in groups for piece in held]
    rows = pieces[0].shape[1]
    sub = rows // n_v
    half_orb = n_orb // 2

    def kernel(index, *refs):
        held = refs[: len(pieces)]
        sides = [
            refs[len(pieces) + side * n_orb : len(pieces) + (side + 1) * n_orb]
            for side in range(2)
        ]
        out, amp, acc = refs[len(pieces) + 2 * n_orb :]
        step = pl.program_id(0)

        @pl.when(step == 0)
        def _():
            base = at = 0
            for group, stored in groups:
                for block in range(count):
                    columns = pl.ds(pl.multiple_of(index[1 + block] * bw, 128), bw)
                    for p in range(len(group)):
                        amp[base + p, :, columns] = held[at][p]
                    at += 1
                base += len(group)

        acc[...] = jnp.zeros_like(acc)

        def add(side, p, i, j):
            acc[i] += jnp.dot(amp[p], sides[side][j][...], preferred_element_type=F32)

        for side in range(2):

            @pl.when((step >= side * steps) & (step < (side + 1) * steps))
            def _(side=side):
                for p, (i, j) in enumerate(pairs):
                    if i == j:
                        add(side, p, i, j)
                    else:
                        flip = index[1 + count + mixed.index((i, j))]

                        @pl.when(flip == 0)
                        def _(p=p, i=i, j=j):
                            add(side, p, i, j)

                        @pl.when(flip != 0)
                        def _(p=p, i=i, j=j):
                            add(side, p, j, i)

        for i in range(n_orb):
            for v in range(n_v):
                out[v, i // half_orb, 0, i % half_orb] = acc[i, v * sub : (v + 1) * sub, :].astype(BF)

    index = jnp.concatenate(
        [jnp.reshape(core, (1,)), blocks] + [jnp.reshape(flips[pair], (1,)) for pair in mixed]
    ).astype(jnp.int32)

    def place(t, index):
        second = (t >= steps).astype(jnp.int32)
        return (0, 0, (index[0] + second) % 2, 0, 0, t - second * steps)

    return call(
        kernel,
        index,
        (*pieces, *[own[o] for o in range(n_orb)], *[sib[o] for o in range(n_orb)]),
        (2 * steps,),
        [pl.BlockSpec(piece.shape, lambda t, index: (0, 0, 0)) for piece in pieces]
        + [pl.BlockSpec((n_virt, tile), lambda t, index: (0, jnp.minimum(t, steps - 1)))] * n_orb
        + [pl.BlockSpec((n_virt, tile), lambda t, index: (0, jnp.maximum(t - steps, 0)))] * n_orb,
        pl.BlockSpec((n_v, 2, 1, half_orb, sub, tile), place),
        jax.ShapeDtypeStruct((n_v, 2, 2, half_orb, sub, width), BF),
        [
            pltpu.VMEM((len(pairs), rows, n_virt), BF),
            pltpu.VMEM((n_orb, rows, tile), F32),
        ],
        cost(
            4 * len(pairs) * rows * n_virt * width,
            4 * n_orb * n_virt * width + 2 * len(pairs) * rows * n_virt,
        ),
        "contract",
    )


def local(pair_list, half_ints, vir_coef, metric, occ_energy, vir_energy):
    n_z, n_v = lax.axis_size("z"), lax.axis_size("v")
    z, v, c, x = (lax.axis_index(name) for name in "zvcx")
    mu_rows, occ_rows, aux = half_ints.shape
    n_virt = vir_coef.shape[1]
    n_orb = 2 * occ_rows
    paired = n_v == 2
    a_rows = n_virt // (2 * n_z)
    sub = a_rows // (2 * n_v)

    def order(value, axis=0):
        shape = value.shape
        split = value.reshape(shape[:axis] + (n_v, 2, n_z, 2, sub) + shape[axis + 1 :])
        perm = [axis + 2, axis + 1, axis + 3, axis, axis + 4]
        rest = list(range(axis + 5, split.ndim))
        return split.transpose(list(range(axis)) + perm + rest).reshape(shape)

    listed = jnp.concatenate([pair_list, swap(pair_list, "x")])
    flips = {
        (i, j): jnp.any((listed[:, 0] == j) & (listed[:, 1] == i)).astype(jnp.int32)
        for i in range(n_orb)
        for j in range(i + 1, n_orb)
    }

    if paired:
        owners = jnp.stack([v * 2 + c, v * 2 + 1 - c, (1 - v) * 2 + c, (1 - v) * 2 + 1 - c])
    else:
        owners = jnp.arange(2 * n_v)

    def fitted_pair(at):
        block = half_ints[:, at, :]
        if paired:
            far = swap(block, "v")
            pieces = [block, swap(block, "c"), far, swap(far, "c")]
        else:
            gathered = lax.all_gather(block, ("v", "c"))
            pieces = [gathered[s] for s in range(2 * n_v)]
        moved = swap(fit(pieces, owners, metric, 1 - x), "x")
        return fit(pieces, owners, metric, x), moved

    def gather_z(value):
        return lax.all_gather(value, "z", axis=0, tiled=True)

    quarter = n_virt // 4
    turned = order(vir_coef.T)
    piece = lax.dynamic_slice_in_dim(turned, (x * 2 + c) * quarter, quarter)
    piece = lax.all_gather(piece, "z", axis=1, tiled=True)
    other = swap(piece, "x")
    coef = jnp.zeros((4, quarter, mu_rows * n_z), BF)
    for part, owner in (
        (piece, x * 2 + c),
        (other, (1 - x) * 2 + c),
        (swap(piece, "c"), x * 2 + 1 - c),
        (swap(other, "c"), (1 - x) * 2 + 1 - c),
    ):
        coef = lax.dynamic_update_slice(coef, part[None], (owner, 0, 0))
    coef = coef.reshape(n_virt, mu_rows * n_z)

    own, sib = {}, {}

    def transform(orbital, held):
        own[orbital] = jnp.dot(coef, held, preferred_element_type=F32).astype(BF)
        sib[orbital] = swap(own[orbital], "c")

    energies = order(vir_energy)
    a_block = z * 2 + c
    if paired:
        blocks = jnp.stack(
            [
                h * 4 + ((x ^ r1) * 2 + (v ^ r2) if h == 0 else (x ^ r2) * 2 + (v ^ r1))
                for h in range(2)
                for r1 in range(2)
                for r2 in range(2)
            ]
        )
        segments = [2] * 4
    else:
        blocks = jnp.arange(2 * n_v)
        segments = [2 * n_v]
    bw = n_virt // blocks.shape[0]

    def amplitude(total, pairs, part, block):
        rows = total.shape[1]
        a = lax.dynamic_slice_in_dim(energies, a_block * a_rows + part * rows, rows)
        b = lax.dynamic_slice_in_dim(energies, block * bw, bw)
        occ = jnp.stack([occ_energy[i] + occ_energy[j] for i, j in pairs])
        denom = (a[None, :, None] + b[None, None, :]) - occ[:, None, None]
        return (-total / denom).astype(BF)

    def reduce_part(segs, pairs, part):
        if not paired:
            total = lax.psum_scatter(segs[0].astype(F32), "v", scatter_dimension=0, tiled=True)
            total = lax.psum_scatter(total, "x", scatter_dimension=0, tiled=True)
            held = amplitude(total[0], pairs, part, v * 2 + x)
            held = lax.all_gather(held, "x")
            held = lax.all_gather(held, "v", axis=0, tiled=True)
            return [held[s] for s in range(2 * n_v)]
        out = []
        for h, (one, two) in enumerate((("x", "v"), ("v", "x"))):
            keep, send = segs[2 * h].astype(F32), segs[2 * h + 1]
            first = swap(send, one).astype(F32)
            second = swap((keep[1] + first[1]).astype(BF), two).astype(F32)
            a00 = amplitude(keep[0] + first[0] + second, pairs, part, h * 4 + x * 2 + v)
            a01 = swap(a00, two)
            a10 = swap(a00, one)
            a11 = swap(a01, one)
            out += [a00, a01, a10, a11]
        return out

    groups = []

    def group(pairs):
        parts = coulomb(own, sib, pairs, flips, blocks, a_block, a_rows, segments)
        groups.append((pairs, [reduce_part(parts[part], pairs, part) for part in range(2)]))

    lower, upper = {}, {}
    for at in range(occ_rows):
        mine, moved = fitted_pair(at)
        if at == 0:
            mine, moved = gather_z(mine), gather_z(moved)
        lower[at] = jnp.where(x == 0, mine, moved)
        upper[at] = jnp.where(x == 0, moved, mine)
        if at > 0:
            lower[at], upper[at] = gather_z(lower[at]), gather_z(upper[at])

    for at in range(occ_rows):
        for orbital, held in ((at, lower[at]), (at + occ_rows, upper[at])):
            seen = list(own)
            transform(orbital, held)
            if at == 0:
                continue
            group([tuple(sorted((s, orbital))) for s in seen] + [(orbital, orbital)])
        if at == 0:
            first, second = own
            group([(first, first), (first, second), (second, second)])

    def exchange(value):
        if not paired:
            value = lax.all_to_all(value, "v", 0, 0, tiled=True)
            value = lax.all_to_all(value, "x", 1, 1, tiled=True)
            return value.transpose(0, 2, 1, 3, 4, 5)

        def take(row, column):
            return lax.dynamic_slice(value, (row, column, 0, 0, 0, 0), (1, 1) + value.shape[2:])[0]

        parts = (
            (take(v, x), v, x),
            (swap(take(v, 1 - x), "x"), v, 1 - x),
            (swap(take(1 - v, x), "v"), 1 - v, x),
            (lax.ppermute(take(1 - v, 1 - x), ("v", "x"), [(k, 3 - k) for k in range(4)]), 1 - v, 1 - x),
        )
        held = jnp.zeros((2, 2, 2) + value.shape[3:], BF)
        for part, row, column in parts:
            held = lax.dynamic_update_slice(
                held, part.transpose(1, 0, 2, 3, 4)[None], (row, 0, column, 0, 0, 0)
            )
        return held

    results = []
    for part in range(2):
        value = contract(
            [(pairs, held[part]) for pairs, held in groups], own, sib, flips, blocks, c, n_v
        )
        value = exchange(value)
        value = value.reshape((n_z, 2 * n_v // n_z) + value.shape[2:])
        results.append(lax.all_to_all(value, "z", 0, 0, tiled=True))
    out = jnp.stack(results).transpose(1, 0, 5, 4, 2, 3, 6)
    return out.astype(F32).reshape(n_virt // (2 * n_v), occ_rows, -1)


def solution(mesh):
    n_ao, n_vir, n_occ = (mesh.shape[name] for name in ("ao", "vir", "occ"))
    fine = Mesh(mesh.devices.reshape(n_ao, n_vir // 2, 2, n_occ), ("z", "v", "c", "x"))
    vir = ("v", "c")
    return jax.shard_map(
        local,
        mesh=fine,
        in_specs=(P("x", None), P("z", "x", vir), P("z", None), P(vir, None), P(), P()),
        out_specs=P(vir, "x", "z"),
        check_vma=False,
    )
```

```python
import functools

import jax
import jax.numpy as jnp
from jax import lax
from jax.experimental import pallas as pl
from jax.experimental.pallas import tpu as pltpu
from jax.sharding import Mesh, PartitionSpec as P

BF = jnp.bfloat16
F32 = jnp.float32
VMEM = 56 * 1024 * 1024
NT = (((1,), (1,)), ((), ()))


def swap(value, axis):
    return lax.ppermute(value, axis, [(0, 1), (1, 0)])


def tile_of(width):
    return 256 if width % 256 == 0 else width


def cost(flops, nbytes):
    return pl.CostEstimate(flops=int(flops), bytes_accessed=int(nbytes), transcendentals=0)


def call(kernel, prefetch, operands, grid, in_specs, out_specs, out_shape, scratch, estimate, name):
    return pl.pallas_call(
        kernel,
        grid_spec=pltpu.PrefetchScalarGridSpec(
            num_scalar_prefetch=1,
            grid=grid,
            in_specs=in_specs,
            out_specs=out_specs,
            scratch_shapes=scratch,
        ),
        out_shape=out_shape,
        compiler_params=pltpu.CompilerParams(vmem_limit_bytes=VMEM),
        cost_estimate=estimate,
        name=name,
    )(prefetch, *operands)


def fit(pieces, owners, metric, half):
    rows, depth = pieces[0].shape
    block, total = metric.shape
    width = block // 2
    tile = tile_of(width)
    steps = width // tile
    count = len(pieces)

    def kernel(index, *refs):
        held, metric_ref, out = refs[:count], refs[count], refs[count + 1]
        acc = None
        for at in range(count):
            columns = pl.ds(pl.multiple_of(index[1 + at] * depth, 128), depth)
            term = lax.dot_general(
                held[at][...], metric_ref[:, columns], NT, preferred_element_type=F32
            )
            acc = term if acc is None else acc + term
        out[...] = acc.astype(BF)

    return call(
        kernel,
        jnp.concatenate([jnp.reshape(half, (1,)), owners]).astype(jnp.int32),
        (*pieces, metric),
        (steps,),
        [pl.BlockSpec((rows, depth), lambda t, index: (0, 0))] * count
        + [pl.BlockSpec((tile, total), lambda t, index: (index[0] * steps + t, 0))],
        pl.BlockSpec((rows, tile), lambda t, index: (0, t)),
        jax.ShapeDtypeStruct((rows, width), BF),
        [],
        cost(2 * rows * total * width, 2 * (rows * total + width * total + rows * width)),
        "fit",
    )


def coulomb(own, sib, pairs, flips, blocks, bw, a_block, rows, segments):
    orbitals = sorted(own)
    n_virt, width = own[orbitals[0]].shape
    count = blocks.shape[0]
    n_orb, n_pairs = len(orbitals), len(pairs)
    n_seg = len(segments)
    mixed = [pair for pair in pairs if pair[0] != pair[1]]

    def kernel(index, *refs):
        left = [refs[at * n_orb : (at + 1) * n_orb] for at in range(2)]
        right = [refs[(2 + at) * n_orb : (3 + at) * n_orb] for at in range(2)]
        outs = refs[4 * n_orb : 4 * n_orb + n_seg]
        acc = refs[4 * n_orb + n_seg]
        step = pl.program_id(0)

        def product(first, second):
            total = None
            for side in range(2):
                term = lax.dot_general(
                    left[side][orbitals.index(first)][...],
                    right[side][orbitals.index(second)][...],
                    NT,
                    preferred_element_type=F32,
                )
                total = term if total is None else total + term
            return total.astype(BF)

        for at, (i, j) in enumerate(pairs):
            if i == j:
                acc[at] = product(i, j)
            else:
                flip = index[1 + count + mixed.index((i, j))]

                @pl.when(flip == 0)
                def _(at=at, i=i, j=j):
                    acc[at] = product(i, j)

                @pl.when(flip != 0)
                def _(at=at, i=i, j=j):
                    acc[at] = product(j, i)

        start = 0
        for seg, length in enumerate(segments):

            @pl.when((step >= start) & (step < start + length))
            def _(seg=seg):
                outs[seg][0] = acc[...]

            start += length

    starts = [sum(segments[:at]) for at in range(n_seg)]
    out_specs = [
        pl.BlockSpec(
            (1, n_pairs, rows, bw),
            lambda t, index, start=start, length=length: (
                jnp.clip(t - start, 0, length - 1),
                0,
                0,
                0,
            ),
        )
        for start, length in zip(starts, segments)
    ]
    out_shape = [
        jax.ShapeDtypeStruct((length, n_pairs, rows, bw), BF) for length in segments
    ]
    arrays = [own[o] for o in orbitals] + [sib[o] for o in orbitals]
    index = jnp.concatenate(
        [jnp.reshape(a_block, (1,)), blocks]
        + [jnp.reshape(flips[pair], (1,)) for pair in mixed]
    ).astype(jnp.int32)
    return call(
        kernel,
        index,
        (*arrays, *arrays),
        (count,),
        [pl.BlockSpec((rows, width), lambda t, index: (index[0], 0))] * (2 * n_orb)
        + [pl.BlockSpec((bw, width), lambda t, index: (index[1 + t], 0))] * (2 * n_orb),
        out_specs,
        out_shape,
        [pltpu.VMEM((n_pairs, rows, bw), BF)],
        cost(
            0.4 * n_pairs * rows * count * bw * width,
            0.4 * n_orb * count * bw * width + 0.2 * n_pairs * rows * count * bw,
        ),
        "coulomb",
    )


def contract(groups, own, sib, flips, blocks, core, n_v, first, steps):
    n_orb = len(own)
    n_virt, width = own[0].shape
    count = blocks.shape[0]
    bw = n_virt // count
    tile = tile_of(width)
    pairs = [pair for group, _ in groups for pair in group]
    mixed = [pair for pair in pairs if pair[0] != pair[1]]
    pieces = [piece for _, held in groups for piece in held]
    rows = pieces[0].shape[1]
    sub = rows // n_v
    half_orb = n_orb // 2

    def kernel(index, *refs):
        held = refs[: len(pieces)]
        sides = [
            refs[len(pieces) + side * n_orb : len(pieces) + (side + 1) * n_orb]
            for side in range(2)
        ]
        out, amp, acc = refs[len(pieces) + 2 * n_orb :]
        step = pl.program_id(0)

        @pl.when(step == 0)
        def _():
            base = at = 0
            for group, _ in groups:
                for block in range(count):
                    columns = pl.ds(pl.multiple_of(index[1 + block] * bw, 128), bw)
                    amp[base : base + len(group), :, columns] = held[at][...]
                    at += 1
                base += len(group)

        for side in range(2):

            @pl.when((step >= side * steps) & (step < (side + 1) * steps))
            def _(side=side):
                def product(p, j):
                    return jnp.dot(amp[p], sides[side][j][...], preferred_element_type=F32)

                for p, (i, j) in enumerate(pairs):
                    if i == j:
                        acc[i] = product(p, i)
                for p, (i, j) in enumerate(pairs):
                    if i != j:
                        flip = index[1 + count + mixed.index((i, j))]

                        @pl.when(flip == 0)
                        def _(p=p, i=i, j=j):
                            acc[i] += product(p, j)

                        @pl.when(flip != 0)
                        def _(p=p, i=i, j=j):
                            acc[j] += product(p, i)

        for i in range(n_orb):
            for v in range(n_v):
                value = acc[i, v * sub : (v + 1) * sub, :]
                out[v, i // half_orb, 0, i % half_orb] = value.astype(BF)

    index = jnp.concatenate(
        [jnp.reshape(core, (1,)), blocks] + [jnp.reshape(flips[pair], (1,)) for pair in mixed]
    ).astype(jnp.int32)

    def place(t, index):
        second = (t >= steps).astype(jnp.int32)
        return (0, 0, (index[0] + second) % 2, 0, 0, t - second * steps)

    return call(
        kernel,
        index,
        (*pieces, *[own[o] for o in range(n_orb)], *[sib[o] for o in range(n_orb)]),
        (2 * steps,),
        [
            pl.BlockSpec(
                piece.shape, lambda t, index: (0, 0, 0), pipeline_mode=pl.Buffered(1)
            )
            for piece in pieces
        ]
        + [
            pl.BlockSpec(
                (n_virt, tile), lambda t, index: (0, first + jnp.minimum(t, steps - 1))
            )
        ]
        * n_orb
        + [pl.BlockSpec((n_virt, tile), lambda t, index: (0, first + jnp.maximum(t - steps, 0)))]
        * n_orb,
        pl.BlockSpec((n_v, 2, 1, half_orb, sub, tile), place),
        jax.ShapeDtypeStruct((n_v, 2, 2, half_orb, sub, steps * tile), BF),
        [
            pltpu.VMEM((len(pairs), rows, n_virt), BF),
            pltpu.VMEM((n_orb, rows, tile), F32),
        ],
        cost(
            4 * len(pairs) * rows * n_virt * steps * tile,
            4 * n_orb * n_virt * steps * tile + 2 * len(pairs) * rows * n_virt,
        ),
        "contract",
    )


def finish(parts):
    n_z, m, n_x, n_i, rows, _ = parts[0].shape
    width = sum(part.shape[-1] for part in parts)
    if width % 128 or rows % 8:
        out = jnp.concatenate(parts, axis=-1).transpose(0, 4, 3, 1, 2, 5)
        return out.astype(F32).reshape(n_z * rows, n_i, m * n_x * width)

    def kernel(*refs):
        out = refs[-1]
        for mm in range(m):
            for xx in range(n_x):
                at = (mm * n_x + xx) * width
                for ref in refs[:-1]:
                    wide = ref.shape[-1]
                    for i in range(n_i):
                        out[:, i, at : at + wide] = ref[0, mm, xx, i].astype(F32)
                    at += wide

    return pl.pallas_call(
        kernel,
        grid=(n_z,),
        in_specs=[
            pl.BlockSpec((1,) + part.shape[1:], lambda z: (z, 0, 0, 0, 0, 0)) for part in parts
        ],
        out_specs=pl.BlockSpec((rows, n_i, m * n_x * width), lambda z: (z, 0, 0)),
        out_shape=jax.ShapeDtypeStruct((n_z * rows, n_i, m * n_x * width), F32),
        compiler_params=pltpu.CompilerParams(vmem_limit_bytes=VMEM),
        name="finish",
    )(*parts)


def after(value, *others):
    return lax.optimization_barrier((value, *others))[0]


def local(pair_list, half_ints, vir_coef, metric, occ_energy, vir_energy):
    n_z, n_v = lax.axis_size("z"), lax.axis_size("v")
    z, v, c, x = (lax.axis_index(name) for name in "zvcx")
    mu_rows, occ_rows, aux = half_ints.shape
    n_virt = vir_coef.shape[1]
    n_orb = 2 * occ_rows
    paired = n_v == 2
    a_rows = n_virt // (2 * n_z)
    sub = a_rows // n_v

    def order(value, axis=0):
        shape = value.shape
        split = value.reshape(shape[:axis] + (n_v, 2, n_z, sub) + shape[axis + 1 :])
        perm = [axis + 2, axis + 1, axis, axis + 3]
        rest = list(range(axis + 4, split.ndim))
        return split.transpose(list(range(axis)) + perm + rest).reshape(shape)

    listed = jnp.concatenate([pair_list, swap(pair_list, "x")])
    flips = {
        (i, j): jnp.any((listed[:, 0] == j) & (listed[:, 1] == i)).astype(jnp.int32)
        for i in range(n_orb)
        for j in range(i + 1, n_orb)
    }

    if paired:
        owners = jnp.stack([v * 2 + c, v * 2 + 1 - c, (1 - v) * 2 + c, (1 - v) * 2 + 1 - c])
    else:
        owners = jnp.arange(2 * n_v)

    def spread(block):
        if paired:
            far = swap(block, "v")
            return [block, swap(block, "c")], far, lambda value: [value, swap(value, "c")]
        gathered = lax.all_gather(block, ("v", "c"))
        return [], gathered, lambda value: [value[s] for s in range(2 * n_v)]

    def gather_z(value, axis=0):
        return lax.all_gather(value, "z", axis=axis, tiled=True)

    part_rows = n_virt // (4 * n_v)
    if paired and part_rows == n_v * sub:
        spot = (c * 2 + v) * 2 + x
        strip = n_virt // (2 * n_v)
        piece = jnp.concatenate(
            [
                lax.dynamic_slice_in_dim(
                    vir_coef, (w * 2 + spot % 2) * strip + spot // 2 * sub, sub, axis=1
                )
                for w in range(n_v)
            ],
            axis=1,
        ).T
        early = piece.reshape(1, part_rows, mu_rows)
        piece = gather_z(early, 2)

        def join(value, axis, low, *others):
            other = after(swap(value, axis), *others)
            return jnp.concatenate(
                [jnp.where(low, value, other), jnp.where(low, other, value)], axis=0
            )

        def coefficients(when):
            held = join(after(piece, *when[0]), "x", x == 0, *when[1])
            held = join(after(held, *when[2]), "v", v == 0, *when[3])
            return join(held, "c", c == 0).reshape(n_virt, mu_rows * n_z)
    else:
        early = vir_coef

        def coefficients(when):
            turned = order(vir_coef.T)
            held = lax.dynamic_slice_in_dim(turned, ((c * n_v + v) * 2 + x) * part_rows, part_rows)
            held = lax.all_gather(gather_z(held, 1), "x", axis=0, tiled=True)
            held = lax.all_gather(held, "v", axis=0, tiled=True)
            return lax.all_gather(held, "c", axis=0, tiled=True)

    own, sib = {}, {}

    def transform(orbital, held, *others):
        own[orbital] = jnp.dot(coef, held, preferred_element_type=F32).astype(BF)
        sib[orbital] = swap(after(own[orbital], *others), "c")

    energies = order(vir_energy)
    a_block = z * 2 + c
    if paired:
        sent, held = (
            jnp.stack(
                [
                    h * 4 + ((x ^ r1) * 2 + (v ^ r2) if h == 0 else (x ^ r2) * 2 + (v ^ r1))
                    for h in range(2)
                    for r2 in range(2)
                ]
            )
            for r1 in (1, 0)
        )
        blocks = jnp.concatenate([held[:2], sent[:2], held[2:], sent[2:]])
    else:
        blocks = jnp.arange(2 * n_v)
    bw = n_virt // blocks.shape[0]

    def amplitude(total, pairs, block):
        a = lax.dynamic_slice_in_dim(energies, a_block * a_rows, a_rows)
        b = lax.dynamic_slice_in_dim(energies, block * bw, bw)
        occ = jnp.stack([occ_energy[i] + occ_energy[j] for i, j in pairs])
        denom = (a[None, :, None] + b[None, None, :]) - occ[:, None, None]
        return (-total / denom).astype(BF)

    groups = []

    def group(pairs, others=()):
        part = functools.partial(coulomb, own, sib, pairs, flips)
        if not paired:
            (total,) = part(blocks, bw, a_block, a_rows, [2 * n_v])
            total = lax.psum_scatter(total.astype(F32), "v", scatter_dimension=0, tiled=True)
            total = lax.psum_scatter(total, "x", scatter_dimension=0, tiled=True)
            piece = lax.all_gather(amplitude(total[0], pairs, v * 2 + x), "x")
            piece = lax.all_gather(piece, "v", axis=0, tiled=True)
            groups.append((pairs, [piece[s] for s in range(2 * n_v)]))
            return [total], [total]
        ways = (("x", "v"), ("v", "x"))
        away = part(sent, bw, a_block, a_rows, [2, 2])
        firsts = [swap(after(away[h], *others), ways[h][0]).astype(F32) for h in range(2)]
        last = {o: after(value, *away) for o, value in own.items()}
        keep = coulomb(last, sib, pairs, flips, held, bw, a_block, a_rows, [2, 2])
        keep = [value.astype(F32) for value in keep]
        seconds = [swap((keep[h][1] + firsts[h][1]).astype(BF), ways[h][1]) for h in range(2)]
        totals = [keep[h][0] + firsts[h][0] + seconds[h].astype(F32) for h in range(2)]
        made = [amplitude(totals[h], pairs, h * 4 + x * 2 + v) for h in range(2)]
        pieces, nears = [], []
        for h in range(2):
            near = swap(made[h], ways[h][1])
            nears.append(near)
            pieces += [made[h], near, swap(made[h], ways[h][0]), swap(near, ways[h][0])]
        groups.append((pairs, pieces))
        return made, nears

    cut = mu_rows // 2
    block = half_ints[:, 0, :]
    near, far, widen = spread(block[:cut])
    near = near + widen(after(far, early))
    mine = [fit(near, owners, metric, x)]
    moved = [fit(near, owners, metric, 1 - x)]
    near, far, widen = spread(after(block[cut:], far))
    near = near + widen(after(far, *mine, *moved))
    mine.append(fit(near, owners, metric, x))
    moved.append(fit(near, owners, metric, 1 - x))
    later = []
    for at in range(1, occ_rows):
        near, far, widen = spread(after(half_ints, far)[:, at, :])
        later.append((near, far, widen, mine[-1], moved[-1]))
    moved = swap(jnp.concatenate(moved), "x")
    shared = jnp.concatenate(
        [gather_z(part).reshape(n_z, cut, -1) for part in mine], axis=1
    ).reshape(mu_rows * n_z, -1)
    following, marks, ready = {}, [], []
    for at in range(1, occ_rows):
        near, far, widen, *others = later[at - 1]
        near = near + widen(after(far, *others))
        here, away = fit(near, owners, metric, x), fit(near, owners, metric, 1 - x)
        marks += [here, away]
        away = swap(after(away, moved), "x")
        chosen = [jnp.where(x == 0, here, away), jnp.where(x == 0, away, here)]
        ready += chosen
        following[at] = [gather_z(value) for value in chosen]
    coef = coefficients((mine[:1], mine[1:], [far], marks))
    moved = gather_z(moved)
    moved = after(moved, *ready)
    transform(0, jnp.where(x == 0, shared, moved))
    transform(occ_rows, jnp.where(x == 0, moved, shared))
    made, nears = group([(0, 0), (0, occ_rows), (occ_rows, occ_rows)])
    for at in range(1, occ_rows):
        for orbital, value in zip((at, at + occ_rows), following[at]):
            seen = list(own)
            transform(orbital, after(value, *made), *nears)
            made, nears = group(
                [tuple(sorted((s, orbital))) for s in seen] + [(orbital, orbital)],
                groups[-1][1],
            )

    def exchange(value, *others):
        if not paired:
            value = lax.all_to_all(value, "v", 0, 0, tiled=True)
            value = lax.all_to_all(value, "x", 1, 1, tiled=True)
            return value.transpose(0, 2, 1, 3, 4, 5)

        def take(row, column):
            return lax.dynamic_slice(value, (row, column, 0, 0, 0, 0), (1, 1) + value.shape[2:])[0]

        parts = (
            (take(v, x), v, x),
            (swap(take(v, 1 - x), "x"), v, 1 - x),
            (swap(take(1 - v, x), "v"), 1 - v, x),
            (lax.ppermute(take(1 - v, 1 - x), ("v", "x"), [(k, 3 - k) for k in range(4)]), 1 - v, 1 - x),
        )
        whole = jnp.zeros((2, 2, 2) + value.shape[3:], BF)
        for part, row, column in parts:
            part = after(part, *others)
            whole = lax.dynamic_update_slice(
                whole, part.transpose(1, 0, 2, 3, 4)[None], (row, 0, column, 0, 0, 0)
            )
        return whole

    made, base = [], own
    for at in range(own[0].shape[1] // tile_of(own[0].shape[1])):
        made.append(contract(groups, base, sib, flips, blocks, c, n_v, at, 1))
        base = {o: after(array, made[-1]) for o, array in base.items()}
    results = []
    for at, value in enumerate(made):
        value = exchange(value, *made[at + 1 : at + 2])
        value = value.reshape((n_z, 2 * n_v // n_z) + value.shape[2:])
        value = after(value, *results[-1:])
        results.append(lax.all_to_all(value, "z", 0, 0, tiled=True))
    return finish(results)


def solution(mesh):
    n_ao, n_vir, n_occ = (mesh.shape[name] for name in ("ao", "vir", "occ"))
    fine = Mesh(mesh.devices.reshape(n_ao, n_vir // 2, 2, n_occ), ("z", "v", "c", "x"))
    vir = ("v", "c")
    return jax.shard_map(
        local,
        mesh=fine,
        in_specs=(P("x", None), P("z", "x", vir), P("z", None), P(vir, None), P(), P()),
        out_specs=P(vir, "x", "z"),
        check_vma=False,
    )
```

```python
import functools

import jax
import jax.numpy as jnp
from jax import lax
from jax.experimental import pallas as pl
from jax.experimental.pallas import tpu as pltpu
from jax.sharding import Mesh, PartitionSpec as P

BF = jnp.bfloat16
F32 = jnp.float32
VMEM = 56 * 1024 * 1024
NT = (((1,), (1,)), ((), ()))


def swap(value, axis):
    return lax.ppermute(value, axis, [(0, 1), (1, 0)])


def tile_of(width):
    return 256 if width % 256 == 0 else width


def cost(flops, nbytes):
    return pl.CostEstimate(flops=int(flops), bytes_accessed=int(nbytes), transcendentals=0)


def call(kernel, prefetch, operands, grid, in_specs, out_specs, out_shape, scratch, estimate, name):
    return pl.pallas_call(
        kernel,
        grid_spec=pltpu.PrefetchScalarGridSpec(
            num_scalar_prefetch=1,
            grid=grid,
            in_specs=in_specs,
            out_specs=out_specs,
            scratch_shapes=scratch,
        ),
        out_shape=out_shape,
        compiler_params=pltpu.CompilerParams(vmem_limit_bytes=VMEM),
        cost_estimate=estimate,
        name=name,
    )(prefetch, *operands)


def fit(pieces, owners, metric, half):
    rows, depth = pieces[0].shape
    block, total = metric.shape
    width = block // 2
    tile = tile_of(width)
    steps = width // tile
    count = len(pieces)

    def kernel(index, *refs):
        held, metric_ref, out = refs[:count], refs[count], refs[count + 1]
        acc = None
        for at in range(count):
            columns = pl.ds(pl.multiple_of(index[1 + at] * depth, 128), depth)
            term = lax.dot_general(
                held[at][...], metric_ref[:, columns], NT, preferred_element_type=F32
            )
            acc = term if acc is None else acc + term
        out[...] = acc.astype(BF)

    return call(
        kernel,
        jnp.concatenate([jnp.reshape(half, (1,)), owners]).astype(jnp.int32),
        (*pieces, metric),
        (steps,),
        [pl.BlockSpec((rows, depth), lambda t, index: (0, 0))] * count
        + [pl.BlockSpec((tile, total), lambda t, index: (index[0] * steps + t, 0))],
        pl.BlockSpec((rows, tile), lambda t, index: (0, t)),
        jax.ShapeDtypeStruct((rows, width), BF),
        [],
        cost(2 * rows * total * width, 2 * (rows * total + width * total + rows * width)),
        "fit",
    )


def coulomb(own, sib, pairs, flips, blocks, bw, a_block, rows, segments):
    orbitals = sorted(own)
    n_virt, width = own[orbitals[0]].shape
    count = blocks.shape[0]
    n_orb, n_pairs = len(orbitals), len(pairs)
    n_seg = len(segments)
    mixed = [pair for pair in pairs if pair[0] != pair[1]]

    def kernel(index, *refs):
        left = [refs[at * n_orb : (at + 1) * n_orb] for at in range(2)]
        right = [refs[(2 + at) * n_orb : (3 + at) * n_orb] for at in range(2)]
        outs = refs[4 * n_orb : 4 * n_orb + n_seg]
        acc = refs[4 * n_orb + n_seg]
        step = pl.program_id(0)

        def product(first, second):
            total = None
            for side in range(2):
                term = lax.dot_general(
                    left[side][orbitals.index(first)][...],
                    right[side][orbitals.index(second)][...],
                    NT,
                    preferred_element_type=F32,
                )
                total = term if total is None else total + term
            return total.astype(BF)

        for at, (i, j) in enumerate(pairs):
            if i == j:
                acc[at] = product(i, j)
            else:
                flip = index[1 + count + mixed.index((i, j))]

                @pl.when(flip == 0)
                def _(at=at, i=i, j=j):
                    acc[at] = product(i, j)

                @pl.when(flip != 0)
                def _(at=at, i=i, j=j):
                    acc[at] = product(j, i)

        start = 0
        for seg, length in enumerate(segments):

            @pl.when((step >= start) & (step < start + length))
            def _(seg=seg):
                outs[seg][0] = acc[...]

            start += length

    starts = [sum(segments[:at]) for at in range(n_seg)]
    out_specs = [
        pl.BlockSpec(
            (1, n_pairs, rows, bw),
            lambda t, index, start=start, length=length: (
                jnp.clip(t - start, 0, length - 1),
                0,
                0,
                0,
            ),
        )
        for start, length in zip(starts, segments)
    ]
    out_shape = [
        jax.ShapeDtypeStruct((length, n_pairs, rows, bw), BF) for length in segments
    ]
    arrays = [own[o] for o in orbitals] + [sib[o] for o in orbitals]
    index = jnp.concatenate(
        [jnp.reshape(a_block, (1,)), blocks]
        + [jnp.reshape(flips[pair], (1,)) for pair in mixed]
    ).astype(jnp.int32)
    return call(
        kernel,
        index,
        (*arrays, *arrays),
        (count,),
        [pl.BlockSpec((rows, width), lambda t, index: (index[0], 0))] * (2 * n_orb)
        + [pl.BlockSpec((bw, width), lambda t, index: (index[1 + t], 0))] * (2 * n_orb),
        out_specs,
        out_shape,
        [pltpu.VMEM((n_pairs, rows, bw), BF)],
        cost(
            0.4 * n_pairs * rows * count * bw * width,
            0.4 * n_orb * count * bw * width + 0.2 * n_pairs * rows * count * bw,
        ),
        "coulomb",
    )


def contract(groups, own, sib, flips, blocks, core, n_v, first, steps, n_orb, base=None, last=True):
    used = sorted({o for group, _ in groups for pair in group for o in pair})
    n_virt, width = own[used[0]].shape
    count = blocks.shape[0]
    bw = n_virt // count
    tile = tile_of(width)
    pairs = [pair for group, _ in groups for pair in group]
    mixed = [pair for pair in pairs if pair[0] != pair[1]]
    pieces = [piece for _, held in groups for piece in held]
    rows = pieces[0].shape[1]
    sub = rows // n_v
    half_orb = n_orb // 2

    def kernel(index, *refs):
        held = refs[: len(pieces)]
        sides = [
            dict(zip(used, refs[len(pieces) + side * len(used) :])) for side in range(2)
        ]
        out, amp, acc = refs[-3:]
        step = pl.program_id(0)

        @pl.when(step == 0)
        def _():
            base = at = 0
            for group, _ in groups:
                for block in range(count):
                    columns = pl.ds(pl.multiple_of(index[1 + block] * bw, 128), bw)
                    amp[base : base + len(group), :, columns] = held[at][...]
                    at += 1
                base += len(group)

        acc[...] = jnp.zeros_like(acc) if base is None else refs[-4][...]

        for side in range(2):

            @pl.when((step >= side * steps) & (step < (side + 1) * steps))
            def _(side=side):
                def product(p, j):
                    return jnp.dot(amp[p], sides[side][j][...], preferred_element_type=F32)

                for p, (i, j) in enumerate(pairs):
                    if i == j:
                        acc[i] += product(p, i)
                    else:
                        flip = index[1 + count + mixed.index((i, j))]

                        @pl.when(flip == 0)
                        def _(p=p, i=i, j=j):
                            acc[i] += product(p, j)

                        @pl.when(flip != 0)
                        def _(p=p, i=i, j=j):
                            acc[j] += product(p, i)

        if not last:
            out[...] = acc[...]
            return
        for i in range(n_orb):
            for v in range(n_v):
                value = acc[i, v * sub : (v + 1) * sub, :]
                out[v, i // half_orb, 0, i % half_orb] = value.astype(BF)

    index = jnp.concatenate(
        [jnp.reshape(core, (1,)), blocks] + [jnp.reshape(flips[pair], (1,)) for pair in mixed]
    ).astype(jnp.int32)

    def place(t, index):
        second = (t >= steps).astype(jnp.int32)
        return (0, 0, (index[0] + second) % 2, 0, 0, t - second * steps)

    stored = steps if base is None else base.shape[0] // 2

    def column(t, index):
        second = (t >= steps).astype(jnp.int32)
        return (first + second * (stored - steps) + t, 0, 0, 0)

    return call(
        kernel,
        index,
        (
            *pieces,
            *[own[o] for o in used],
            *[sib[o] for o in used],
            *([] if base is None else [base]),
        ),
        (2 * steps,),
        [
            pl.BlockSpec(
                piece.shape, lambda t, index: (0, 0, 0), pipeline_mode=pl.Buffered(1)
            )
            for piece in pieces
        ]
        + [
            pl.BlockSpec(
                (n_virt, tile), lambda t, index: (0, first + jnp.minimum(t, steps - 1))
            )
        ]
        * len(used)
        + [pl.BlockSpec((n_virt, tile), lambda t, index: (0, first + jnp.maximum(t - steps, 0)))]
        * len(used)
        + ([] if base is None else [pl.BlockSpec((None, n_orb, rows, tile), column)]),
        pl.BlockSpec((n_v, 2, 1, half_orb, sub, tile), place)
        if last
        else pl.BlockSpec((None, n_orb, rows, tile), column),
        jax.ShapeDtypeStruct((n_v, 2, 2, half_orb, sub, steps * tile), BF)
        if last
        else jax.ShapeDtypeStruct((2 * steps, n_orb, rows, tile), F32),
        [
            pltpu.VMEM((len(pairs), rows, n_virt), BF),
            pltpu.VMEM((n_orb, rows, tile), F32),
        ],
        cost(
            4 * len(pairs) * rows * n_virt * steps * tile,
            4 * len(used) * n_virt * steps * tile + 2 * len(pairs) * rows * n_virt,
        ),
        "contract",
    )


def finish(parts):
    n_z, m, n_x, n_i, rows, _ = parts[0].shape
    width = sum(part.shape[-1] for part in parts)
    if width % 128 or rows % 8:
        out = jnp.concatenate(parts, axis=-1).transpose(0, 4, 3, 1, 2, 5)
        return out.astype(F32).reshape(n_z * rows, n_i, m * n_x * width)

    def kernel(*refs):
        out = refs[-1]
        for mm in range(m):
            for xx in range(n_x):
                at = (mm * n_x + xx) * width
                for ref in refs[:-1]:
                    wide = ref.shape[-1]
                    for i in range(n_i):
                        out[:, i, at : at + wide] = ref[0, mm, xx, i].astype(F32)
                    at += wide

    return pl.pallas_call(
        kernel,
        grid=(n_z,),
        in_specs=[
            pl.BlockSpec((1,) + part.shape[1:], lambda z: (z, 0, 0, 0, 0, 0)) for part in parts
        ],
        out_specs=pl.BlockSpec((rows, n_i, m * n_x * width), lambda z: (z, 0, 0)),
        out_shape=jax.ShapeDtypeStruct((n_z * rows, n_i, m * n_x * width), F32),
        compiler_params=pltpu.CompilerParams(vmem_limit_bytes=VMEM),
        name="finish",
    )(*parts)


def after(value, *others):
    return lax.optimization_barrier((value, *others))[0]


def local(pair_list, half_ints, vir_coef, metric, occ_energy, vir_energy):
    n_z, n_v = lax.axis_size("z"), lax.axis_size("v")
    z, v, c, x = (lax.axis_index(name) for name in "zvcx")
    mu_rows, occ_rows, aux = half_ints.shape
    n_virt = vir_coef.shape[1]
    n_orb = 2 * occ_rows
    paired = n_v == 2
    a_rows = n_virt // (2 * n_z)
    sub = a_rows // n_v

    def order(value, axis=0):
        shape = value.shape
        split = value.reshape(shape[:axis] + (n_v, 2, n_z, sub) + shape[axis + 1 :])
        perm = [axis + 2, axis + 1, axis, axis + 3]
        rest = list(range(axis + 4, split.ndim))
        return split.transpose(list(range(axis)) + perm + rest).reshape(shape)

    listed = jnp.concatenate([pair_list, swap(pair_list, "x")])
    flips = {
        (i, j): jnp.any((listed[:, 0] == j) & (listed[:, 1] == i)).astype(jnp.int32)
        for i in range(n_orb)
        for j in range(i + 1, n_orb)
    }

    if paired:
        owners = jnp.stack([v * 2 + c, v * 2 + 1 - c, (1 - v) * 2 + c, (1 - v) * 2 + 1 - c])
    else:
        owners = jnp.arange(2 * n_v)

    def spread(block):
        if paired:
            far = swap(block, "v")
            return [block, swap(block, "c")], far, lambda value: [value, swap(value, "c")]
        gathered = lax.all_gather(block, ("v", "c"))
        return [], gathered, lambda value: [value[s] for s in range(2 * n_v)]

    def gather_z(value, axis=0):
        return lax.all_gather(value, "z", axis=axis, tiled=True)

    part_rows = n_virt // (4 * n_v)
    if paired and part_rows == n_v * sub:
        spot = (c * 2 + v) * 2 + x
        strip = n_virt // (2 * n_v)
        piece = jnp.concatenate(
            [
                lax.dynamic_slice_in_dim(
                    vir_coef, (w * 2 + spot % 2) * strip + spot // 2 * sub, sub, axis=1
                )
                for w in range(n_v)
            ],
            axis=1,
        ).T
        early = piece.reshape(1, part_rows, mu_rows)
        piece = gather_z(early, 2)

        def join(value, axis, low, *others):
            other = after(swap(value, axis), *others)
            return jnp.concatenate(
                [jnp.where(low, value, other), jnp.where(low, other, value)], axis=0
            )

        def coefficients(when):
            held = join(after(piece, *when[0]), "x", x == 0, *when[1])
            held = join(after(held, *when[2]), "v", v == 0, *when[3])
            return join(held, "c", c == 0).reshape(n_virt, mu_rows * n_z)
    else:
        early = vir_coef

        def coefficients(when):
            turned = order(vir_coef.T)
            held = lax.dynamic_slice_in_dim(turned, ((c * n_v + v) * 2 + x) * part_rows, part_rows)
            held = lax.all_gather(gather_z(held, 1), "x", axis=0, tiled=True)
            held = lax.all_gather(held, "v", axis=0, tiled=True)
            return lax.all_gather(held, "c", axis=0, tiled=True)

    own, sib = {}, {}

    def transform(orbital, held, *others):
        own[orbital] = jnp.dot(coef, held, preferred_element_type=F32).astype(BF)
        sib[orbital] = swap(after(own[orbital], *others), "c")

    energies = order(vir_energy)
    a_block = z * 2 + c
    if paired:
        sent, held = (
            jnp.stack(
                [
                    h * 4 + ((x ^ r1) * 2 + (v ^ r2) if h == 0 else (x ^ r2) * 2 + (v ^ r1))
                    for h in range(2)
                    for r2 in range(2)
                ]
            )
            for r1 in (1, 0)
        )
        blocks = jnp.concatenate([held[:2], sent[:2], held[2:], sent[2:]])
    else:
        blocks = jnp.arange(2 * n_v)
    bw = n_virt // blocks.shape[0]

    def amplitude(total, pairs, block):
        a = lax.dynamic_slice_in_dim(energies, a_block * a_rows, a_rows)
        b = lax.dynamic_slice_in_dim(energies, block * bw, bw)
        occ = jnp.stack([occ_energy[i] + occ_energy[j] for i, j in pairs])
        denom = (a[None, :, None] + b[None, None, :]) - occ[:, None, None]
        return (-total / denom).astype(BF)

    groups = []

    def group(pairs, others=(), fill=()):
        part = functools.partial(coulomb, own, sib, pairs, flips)
        if not paired:
            (total,) = part(blocks, bw, a_block, a_rows, [2 * n_v])
            total = lax.psum_scatter(total.astype(F32), "v", scatter_dimension=0, tiled=True)
            total = lax.psum_scatter(total, "x", scatter_dimension=0, tiled=True)
            piece = lax.all_gather(amplitude(total[0], pairs, v * 2 + x), "x")
            piece = lax.all_gather(piece, "v", axis=0, tiled=True)
            groups.append((pairs, [piece[s] for s in range(2 * n_v)]))
            return [total], [total]
        ways = (("x", "v"), ("v", "x"))
        away = part(sent, bw, a_block, a_rows, [2, 2])
        firsts = [swap(after(away[h], *others), ways[h][0]).astype(F32) for h in range(2)]
        last = {o: after(value, *away) for o, value in own.items()}
        keep = coulomb(last, sib, pairs, flips, held, bw, a_block, a_rows, [2, 2])
        keep = [value.astype(F32) for value in keep]
        seconds = [swap((keep[h][1] + firsts[h][1]).astype(BF), ways[h][1]) for h in range(2)]
        totals = [keep[h][0] + firsts[h][0] + seconds[h].astype(F32) for h in range(2)]
        made = [amplitude(totals[h], pairs, h * 4 + x * 2 + v) for h in range(2)]
        pieces, nears = [], []
        for h in range(2):
            near = swap(made[h], ways[h][1])
            nears.append(near)
            direct = swap(made[h], ways[h][0])
            far = swap(after(near, *fill, *([direct] if fill else [])), ways[h][0])
            pieces += [made[h], near, direct, far]
        groups.append((pairs, pieces))
        return made, nears

    half = metric.shape[0] // 2
    steps = half // tile_of(half)

    cut = mu_rows // 2
    block = half_ints[:, 0, :]
    near, far, widen = spread(block[:cut])
    near = near + widen(after(far, early))
    mine = [fit(near, owners, metric, x)]
    moved = [fit(near, owners, metric, 1 - x)]
    near, far, widen = spread(after(block[cut:], far))
    near = near + widen(after(far, *mine, *moved))
    mine.append(fit(near, owners, metric, x))
    moved.append(fit(near, owners, metric, 1 - x))
    later = []
    for at in range(1, occ_rows):
        near, far, widen = spread(after(half_ints, far)[:, at, :])
        later.append((near, far, widen, mine[-1], moved[-1]))
    moved = swap(jnp.concatenate(moved), "x")
    shared = jnp.concatenate(
        [gather_z(part).reshape(n_z, cut, -1) for part in mine], axis=1
    ).reshape(mu_rows * n_z, -1)
    following, marks, ready = {}, [], []
    for at in range(1, occ_rows):
        near, far, widen, *others = later[at - 1]
        near = near + widen(after(far, *others))
        here, away = fit(near, owners, metric, x), fit(near, owners, metric, 1 - x)
        marks += [here, away]
        away = swap(after(away, moved), "x")
        chosen = [jnp.where(x == 0, here, away), jnp.where(x == 0, away, here)]
        ready += chosen
        following[at] = [gather_z(value) for value in chosen]
    coef = coefficients((mine[:1], mine[1:], [far], marks))
    moved = gather_z(moved)
    transform(0, shared)
    transform(occ_rows, after(moved, *ready, own[0]))
    for side in (own, sib):
        here, away = side[0], side[occ_rows]
        side[0] = jnp.where(x == 0, here, away)
        side[occ_rows] = jnp.where(x == 0, away, here)
    sums = []
    made, nears = group([(0, 0), (0, occ_rows), (occ_rows, occ_rows)])
    for at in range(1, occ_rows):
        for orbital, value in zip((at, at + occ_rows), following[at]):
            seen = list(own)
            transform(orbital, after(value, *made), *nears)
            if len(own) == n_orb:
                wide = max(1, steps - 1)
                sums.append(
                    contract(groups[:], own, sib, flips, blocks, c, n_v, 0, wide, n_orb, last=False)
                )
            made, nears = group(
                [tuple(sorted((s, orbital))) for s in seen] + [(orbital, orbital)],
                groups[-1][1],
                tuple(sums),
            )

    def exchange(value, *others):
        if not paired:
            value = lax.all_to_all(value, "v", 0, 0, tiled=True)
            value = lax.all_to_all(value, "x", 1, 1, tiled=True)
            return value.transpose(0, 2, 1, 3, 4, 5)

        def take(row, column):
            return lax.dynamic_slice(value, (row, column, 0, 0, 0, 0), (1, 1) + value.shape[2:])[0]

        parts = (
            (take(v, x), v, x),
            (swap(take(v, 1 - x), "x"), v, 1 - x),
            (swap(take(1 - v, x), "v"), 1 - v, x),
            (lax.ppermute(take(1 - v, 1 - x), ("v", "x"), [(k, 3 - k) for k in range(4)]), 1 - v, 1 - x),
        )
        near, beside, above, across = (after(part, *others)[0] for part, _, _ in parts)
        mine = [jnp.where(x == 0, near, beside), jnp.where(x == 0, beside, near)]
        other = [jnp.where(x == 0, above, across), jnp.where(x == 0, across, above)]
        mine, other = jnp.stack(mine, axis=1), jnp.stack(other, axis=1)
        return jnp.stack([jnp.where(v == 0, mine, other), jnp.where(v == 0, other, mine)])

    results = []
    made, held = [], own
    for at in range(steps):
        chosen, base = (groups[-1:], sums[0]) if at < wide else (groups, None)
        made.append(contract(chosen, held, sib, flips, blocks, c, n_v, at, 1, n_orb, base))
        held = {o: after(array, made[-1]) for o, array in held.items()}
    for at, value in enumerate(made):
        value = exchange(value, *made[at + 1 : at + 2])
        value = value.reshape((n_z, 2 * n_v // n_z) + value.shape[2:])
        value = after(value, *results[-1:])
        results.append(lax.all_to_all(value, "z", 0, 0, tiled=True))
    return finish(results)


def solution(mesh):
    n_ao, n_vir, n_occ = (mesh.shape[name] for name in ("ao", "vir", "occ"))
    fine = Mesh(mesh.devices.reshape(n_ao, n_vir // 2, 2, n_occ), ("z", "v", "c", "x"))
    vir = ("v", "c")
    return jax.shard_map(
        local,
        mesh=fine,
        in_specs=(P("x", None), P("z", "x", vir), P("z", None), P(vir, None), P(), P()),
        out_specs=P(vir, "x", "z"),
        check_vma=False,
    )
```

```python
import functools

import jax
import jax.numpy as jnp
from jax import lax
from jax.experimental import pallas as pl
from jax.experimental.pallas import tpu as pltpu
from jax.sharding import Mesh, PartitionSpec as P

BF = jnp.bfloat16
F32 = jnp.float32
VMEM = 56 * 1024 * 1024
NT = (((1,), (1,)), ((), ()))


def swap(value, axis):
    return lax.ppermute(value, axis, [(0, 1), (1, 0)])


def tile_of(width):
    return 256 if width % 256 == 0 else width


def cost(flops, nbytes):
    return pl.CostEstimate(flops=int(flops), bytes_accessed=int(nbytes), transcendentals=0)


def call(kernel, prefetch, operands, grid, in_specs, out_specs, out_shape, scratch, estimate, name):
    return pl.pallas_call(
        kernel,
        grid_spec=pltpu.PrefetchScalarGridSpec(
            num_scalar_prefetch=1,
            grid=grid,
            in_specs=in_specs,
            out_specs=out_specs,
            scratch_shapes=scratch,
        ),
        out_shape=out_shape,
        compiler_params=pltpu.CompilerParams(vmem_limit_bytes=VMEM),
        cost_estimate=estimate,
        name=name,
    )(prefetch, *operands)


def fit(pieces, owners, metric, half):
    rows, depth = pieces[0].shape
    block, total = metric.shape
    width = block // 2
    tile = tile_of(width)
    steps = width // tile
    count = len(pieces)

    def kernel(index, *refs):
        held, metric_ref, out = refs[:count], refs[count], refs[count + 1]
        acc = None
        for at in range(count):
            columns = pl.ds(pl.multiple_of(index[1 + at] * depth, 128), depth)
            term = lax.dot_general(
                held[at][...], metric_ref[:, columns], NT, preferred_element_type=F32
            )
            acc = term if acc is None else acc + term
        out[...] = acc.astype(BF)

    return call(
        kernel,
        jnp.concatenate([jnp.reshape(half, (1,)), owners]).astype(jnp.int32),
        (*pieces, metric),
        (steps,),
        [pl.BlockSpec((rows, depth), lambda t, index: (0, 0))] * count
        + [pl.BlockSpec((tile, total), lambda t, index: (index[0] * steps + t, 0))],
        pl.BlockSpec((rows, tile), lambda t, index: (0, t)),
        jax.ShapeDtypeStruct((rows, width), BF),
        [],
        cost(2 * rows * total * width, 2 * (rows * total + width * total + rows * width)),
        "fit",
    )


def coulomb(own, sib, pairs, flips, blocks, bw, a_block, rows, segments):
    orbitals = sorted(own)
    n_virt, width = own[orbitals[0]].shape
    count = blocks.shape[0]
    n_orb, n_pairs = len(orbitals), len(pairs)
    n_seg = len(segments)
    mixed = [pair for pair in pairs if pair[0] != pair[1]]

    def kernel(index, *refs):
        left = [refs[at * n_orb : (at + 1) * n_orb] for at in range(2)]
        right = [refs[(2 + at) * n_orb : (3 + at) * n_orb] for at in range(2)]
        outs = refs[4 * n_orb : 4 * n_orb + n_seg]
        acc = refs[4 * n_orb + n_seg]
        step = pl.program_id(0)

        def product(first, second):
            total = None
            for side in range(2):
                term = lax.dot_general(
                    left[side][orbitals.index(first)][...],
                    right[side][orbitals.index(second)][...],
                    NT,
                    preferred_element_type=F32,
                )
                total = term if total is None else total + term
            return total.astype(BF)

        for at, (i, j) in enumerate(pairs):
            if i == j:
                acc[at] = product(i, j)
            else:
                flip = index[1 + count + mixed.index((i, j))]

                @pl.when(flip == 0)
                def _(at=at, i=i, j=j):
                    acc[at] = product(i, j)

                @pl.when(flip != 0)
                def _(at=at, i=i, j=j):
                    acc[at] = product(j, i)

        start = 0
        for seg, length in enumerate(segments):

            @pl.when((step >= start) & (step < start + length))
            def _(seg=seg):
                outs[seg][0] = acc[...]

            start += length

    starts = [sum(segments[:at]) for at in range(n_seg)]
    out_specs = [
        pl.BlockSpec(
            (1, n_pairs, rows, bw),
            lambda t, index, start=start, length=length: (
                jnp.clip(t - start, 0, length - 1),
                0,
                0,
                0,
            ),
        )
        for start, length in zip(starts, segments)
    ]
    out_shape = [
        jax.ShapeDtypeStruct((length, n_pairs, rows, bw), BF) for length in segments
    ]
    arrays = [own[o] for o in orbitals] + [sib[o] for o in orbitals]
    index = jnp.concatenate(
        [jnp.reshape(a_block, (1,)), blocks]
        + [jnp.reshape(flips[pair], (1,)) for pair in mixed]
    ).astype(jnp.int32)
    return call(
        kernel,
        index,
        (*arrays, *arrays),
        (count,),
        [pl.BlockSpec((rows, width), lambda t, index: (index[0], 0))] * (2 * n_orb)
        + [pl.BlockSpec((bw, width), lambda t, index: (index[1 + t], 0))] * (2 * n_orb),
        out_specs,
        out_shape,
        [pltpu.VMEM((n_pairs, rows, bw), BF)],
        cost(
            0.4 * n_pairs * rows * count * bw * width,
            0.4 * n_orb * count * bw * width + 0.2 * n_pairs * rows * count * bw,
        ),
        "coulomb",
    )


def contract(groups, own, sib, flips, blocks, core, n_v, first, steps, n_orb, base=None, last=True):
    used = sorted({o for group, _ in groups for pair in group for o in pair})
    n_virt, width = own[used[0]].shape
    count = blocks.shape[0]
    bw = n_virt // count
    tile = tile_of(width)
    pairs = [pair for group, _ in groups for pair in group]
    mixed = [pair for pair in pairs if pair[0] != pair[1]]
    pieces = [piece for _, held in groups for piece in held]
    rows = pieces[0].shape[1]
    sub = rows // n_v
    half_orb = n_orb // 2

    def kernel(index, *refs):
        held = refs[: len(pieces)]
        sides = [
            dict(zip(used, refs[len(pieces) + side * len(used) :])) for side in range(2)
        ]
        out, amp, acc = refs[-3:]
        step = pl.program_id(0)

        @pl.when(step == 0)
        def _():
            base = at = 0
            for group, _ in groups:
                for block in range(count):
                    columns = pl.ds(pl.multiple_of(index[1 + block] * bw, 128), bw)
                    amp[base : base + len(group), :, columns] = held[at][...]
                    at += 1
                base += len(group)

        acc[...] = jnp.zeros_like(acc) if base is None else refs[-4][...]

        for side in range(2):

            @pl.when((step >= side * steps) & (step < (side + 1) * steps))
            def _(side=side):
                def product(p, j):
                    return jnp.dot(amp[p], sides[side][j][...], preferred_element_type=F32)

                for p, (i, j) in enumerate(pairs):
                    if i == j:
                        acc[i] += product(p, i)
                    else:
                        flip = index[1 + count + mixed.index((i, j))]

                        @pl.when(flip == 0)
                        def _(p=p, i=i, j=j):
                            acc[i] += product(p, j)

                        @pl.when(flip != 0)
                        def _(p=p, i=i, j=j):
                            acc[j] += product(p, i)

        if not last:
            out[...] = acc[...]
            return
        for i in range(n_orb):
            for v in range(n_v):
                value = acc[i, v * sub : (v + 1) * sub, :]
                out[v, i // half_orb, 0, i % half_orb] = value.astype(BF)

    index = jnp.concatenate(
        [jnp.reshape(core, (1,)), blocks] + [jnp.reshape(flips[pair], (1,)) for pair in mixed]
    ).astype(jnp.int32)

    def place(t, index):
        second = (t >= steps).astype(jnp.int32)
        return (0, 0, (index[0] + second) % 2, 0, 0, t - second * steps)

    stored = steps if base is None else base.shape[0] // 2

    def column(t, index):
        second = (t >= steps).astype(jnp.int32)
        return (first + second * (stored - steps) + t, 0, 0, 0)

    return call(
        kernel,
        index,
        (
            *pieces,
            *[own[o] for o in used],
            *[sib[o] for o in used],
            *([] if base is None else [base]),
        ),
        (2 * steps,),
        [
            pl.BlockSpec(
                piece.shape, lambda t, index: (0, 0, 0), pipeline_mode=pl.Buffered(1)
            )
            for piece in pieces
        ]
        + [
            pl.BlockSpec(
                (n_virt, tile), lambda t, index: (0, first + jnp.minimum(t, steps - 1))
            )
        ]
        * len(used)
        + [pl.BlockSpec((n_virt, tile), lambda t, index: (0, first + jnp.maximum(t - steps, 0)))]
        * len(used)
        + ([] if base is None else [pl.BlockSpec((None, n_orb, rows, tile), column)]),
        pl.BlockSpec((n_v, 2, 1, half_orb, sub, tile), place)
        if last
        else pl.BlockSpec((None, n_orb, rows, tile), column),
        jax.ShapeDtypeStruct((n_v, 2, 2, half_orb, sub, steps * tile), BF)
        if last
        else jax.ShapeDtypeStruct((2 * steps, n_orb, rows, tile), F32),
        [
            pltpu.VMEM((len(pairs), rows, n_virt), BF),
            pltpu.VMEM((n_orb, rows, tile), F32),
        ],
        cost(
            4 * len(pairs) * rows * n_virt * steps * tile,
            4 * len(used) * n_virt * steps * tile + 2 * len(pairs) * rows * n_virt,
        ),
        "contract",
    )


def finish(parts):
    n_z, m, n_x, n_i, rows, _ = parts[0].shape
    width = sum(part.shape[-1] for part in parts)
    if width % 128 or rows % 8:
        out = jnp.concatenate(parts, axis=-1).transpose(0, 4, 3, 1, 2, 5)
        return out.astype(F32).reshape(n_z * rows, n_i, m * n_x * width)

    def kernel(*refs):
        out = refs[-1]
        for mm in range(m):
            for xx in range(n_x):
                at = (mm * n_x + xx) * width
                for ref in refs[:-1]:
                    wide = ref.shape[-1]
                    for i in range(n_i):
                        out[:, i, at : at + wide] = ref[0, mm, xx, i].astype(F32)
                    at += wide

    return pl.pallas_call(
        kernel,
        grid=(n_z,),
        in_specs=[
            pl.BlockSpec((1,) + part.shape[1:], lambda z: (z, 0, 0, 0, 0, 0)) for part in parts
        ],
        out_specs=pl.BlockSpec((rows, n_i, m * n_x * width), lambda z: (z, 0, 0)),
        out_shape=jax.ShapeDtypeStruct((n_z * rows, n_i, m * n_x * width), F32),
        compiler_params=pltpu.CompilerParams(vmem_limit_bytes=VMEM),
        name="finish",
    )(*parts)


def after(value, *others):
    return lax.optimization_barrier((value, *others))[0]


def local(pair_list, half_ints, vir_coef, metric, occ_energy, vir_energy):
    n_z, n_v = lax.axis_size("z"), lax.axis_size("v")
    z, v, c, x = (lax.axis_index(name) for name in "zvcx")
    mu_rows, occ_rows, aux = half_ints.shape
    n_virt = vir_coef.shape[1]
    n_orb = 2 * occ_rows
    paired = n_v == 2
    a_rows = n_virt // (2 * n_z)
    sub = a_rows // n_v

    def order(value, axis=0):
        shape = value.shape
        split = value.reshape(shape[:axis] + (n_v, 2, n_z, sub) + shape[axis + 1 :])
        perm = [axis + 2, axis + 1, axis, axis + 3]
        rest = list(range(axis + 4, split.ndim))
        return split.transpose(list(range(axis)) + perm + rest).reshape(shape)

    listed = jnp.concatenate([pair_list, swap(pair_list, "x")])
    flips = {
        (i, j): jnp.any((listed[:, 0] == j) & (listed[:, 1] == i)).astype(jnp.int32)
        for i in range(n_orb)
        for j in range(i + 1, n_orb)
    }

    if paired:
        owners = jnp.stack([v * 2 + c, v * 2 + 1 - c, (1 - v) * 2 + c, (1 - v) * 2 + 1 - c])
    else:
        owners = jnp.arange(2 * n_v)

    def spread(block):
        if paired:
            far = swap(block, "v")
            return [block, swap(block, "c")], far, lambda value: [value, swap(value, "c")]
        gathered = lax.all_gather(block, ("v", "c"))
        return [], gathered, lambda value: [value[s] for s in range(2 * n_v)]

    def gather_z(value, axis=0):
        return lax.all_gather(value, "z", axis=axis, tiled=True)

    part_rows = n_virt // (4 * n_v)
    if paired and part_rows == n_v * sub:
        spot = (c * 2 + v) * 2 + x
        strip = n_virt // (2 * n_v)
        piece = jnp.concatenate(
            [
                lax.dynamic_slice_in_dim(
                    vir_coef, (w * 2 + spot % 2) * strip + spot // 2 * sub, sub, axis=1
                )
                for w in range(n_v)
            ],
            axis=1,
        ).T
        early = piece.reshape(1, part_rows, mu_rows)
        piece = gather_z(early, 2)

        def join(value, axis, low, *others):
            other = after(swap(value, axis), *others)
            return jnp.concatenate(
                [jnp.where(low, value, other), jnp.where(low, other, value)], axis=0
            )

        def coefficients(when):
            held = join(after(piece, *when[0]), "x", x == 0, *when[1])
            held = join(after(held, *when[2]), "v", v == 0, *when[3])
            return join(held, "c", c == 0).reshape(n_virt, mu_rows * n_z)
    else:
        early = vir_coef

        def coefficients(when):
            turned = order(vir_coef.T)
            held = lax.dynamic_slice_in_dim(turned, ((c * n_v + v) * 2 + x) * part_rows, part_rows)
            held = lax.all_gather(gather_z(held, 1), "x", axis=0, tiled=True)
            held = lax.all_gather(held, "v", axis=0, tiled=True)
            return lax.all_gather(held, "c", axis=0, tiled=True)

    own, sib = {}, {}

    def transform(orbital, held, *others):
        own[orbital] = jnp.dot(coef, held, preferred_element_type=F32).astype(BF)
        sib[orbital] = swap(after(own[orbital], *others), "c")

    energies = order(vir_energy)
    a_block = z * 2 + c
    if paired:
        sent, held = (
            jnp.stack(
                [
                    h * 4 + ((x ^ r1) * 2 + (v ^ r2) if h == 0 else (x ^ r2) * 2 + (v ^ r1))
                    for h in range(2)
                    for r2 in range(2)
                ]
            )
            for r1 in (1, 0)
        )
        blocks = jnp.concatenate([held[:2], sent[:2], held[2:], sent[2:]])
    else:
        blocks = jnp.arange(2 * n_v)
    bw = n_virt // blocks.shape[0]

    def amplitude(total, pairs, block):
        a = lax.dynamic_slice_in_dim(energies, a_block * a_rows, a_rows)
        b = lax.dynamic_slice_in_dim(energies, block * bw, bw)
        occ = jnp.stack([occ_energy[i] + occ_energy[j] for i, j in pairs])
        denom = (a[None, :, None] + b[None, None, :]) - occ[:, None, None]
        return (-total / denom).astype(BF)

    groups = []

    def group(pairs, others=(), fill=()):
        part = functools.partial(coulomb, own, sib, pairs, flips)
        if not paired:
            (total,) = part(blocks, bw, a_block, a_rows, [2 * n_v])
            total = lax.psum_scatter(total.astype(F32), "v", scatter_dimension=0, tiled=True)
            total = lax.psum_scatter(total, "x", scatter_dimension=0, tiled=True)
            piece = lax.all_gather(amplitude(total[0], pairs, v * 2 + x), "x")
            piece = lax.all_gather(piece, "v", axis=0, tiled=True)
            groups.append((pairs, [piece[s] for s in range(2 * n_v)]))
            return [total], [total]
        ways = (("x", "v"), ("v", "x"))
        away = part(sent, bw, a_block, a_rows, [2, 2])
        firsts = [swap(after(away[h], *others), ways[h][0]).astype(F32) for h in range(2)]
        last = {o: after(value, *away) for o, value in own.items()}
        keep = coulomb(last, sib, pairs, flips, held, bw, a_block, a_rows, [2, 2])
        keep = [value.astype(F32) for value in keep]
        seconds = [swap((keep[h][1] + firsts[h][1]).astype(BF), ways[h][1]) for h in range(2)]
        totals = [keep[h][0] + firsts[h][0] + seconds[h].astype(F32) for h in range(2)]
        made = [amplitude(totals[h], pairs, h * 4 + x * 2 + v) for h in range(2)]
        pieces, nears = [], []
        for h in range(2):
            near = swap(made[h], ways[h][1])
            nears.append(near)
            direct = swap(made[h], ways[h][0])
            far = swap(after(near, *fill, *([direct] if fill else [])), ways[h][0])
            pieces += [made[h], near, direct, far]
        groups.append((pairs, pieces))
        return made, nears

    half = metric.shape[0] // 2
    steps = half // tile_of(half)

    cut = mu_rows // 2
    block = half_ints[:, 0, :]
    near, far, widen = spread(block[:cut])
    near = near + widen(after(far, early))
    mine = [fit(near, owners, metric, x)]
    moved = [fit(near, owners, metric, 1 - x)]
    near, far, widen = spread(after(block[cut:], far))
    near = near + widen(after(far, *mine, *moved))
    mine.append(fit(near, owners, metric, x))
    moved.append(fit(near, owners, metric, 1 - x))
    later = []
    for at in range(1, occ_rows):
        near, far, widen = spread(after(half_ints, far)[:, at, :])
        later.append((near, far, widen, mine[-1], moved[-1]))
    moved = swap(jnp.concatenate(moved), "x")
    shared = jnp.concatenate(
        [gather_z(part).reshape(n_z, cut, -1) for part in mine], axis=1
    ).reshape(mu_rows * n_z, -1)
    following, marks, ready = {}, [], []
    for at in range(1, occ_rows):
        near, far, widen, *others = later[at - 1]
        near = near + widen(after(far, *others))
        here, away = fit(near, owners, metric, x), fit(near, owners, metric, 1 - x)
        marks += [here, away]
        away = swap(after(away, moved), "x")
        chosen = [jnp.where(x == 0, here, away), jnp.where(x == 0, away, here)]
        ready += chosen
        following[at] = [gather_z(value) for value in chosen]
    coef = coefficients((mine[:1], mine[1:], [far], marks))
    moved = gather_z(moved)
    transform(0, shared)
    transform(occ_rows, after(moved, *ready, own[0]))
    for side in (own, sib):
        here, away = side[0], side[occ_rows]
        side[0] = jnp.where(x == 0, here, away)
        side[occ_rows] = jnp.where(x == 0, away, here)
    sums = []
    made, nears = group([(0, 0), (0, occ_rows), (occ_rows, occ_rows)])
    for at in range(1, occ_rows):
        for orbital, value in zip((at, at + occ_rows), following[at]):
            seen = list(own)
            transform(orbital, after(value, *made), *nears)
            if len(own) == n_orb:
                wide = max(1, steps - 1)
                sums.append(
                    contract(groups[:], own, sib, flips, blocks, c, n_v, 0, wide, n_orb, last=False)
                )
            made, nears = group(
                [tuple(sorted((s, orbital))) for s in seen] + [(orbital, orbital)],
                groups[-1][1],
                tuple(sums),
            )

    def exchange(value, *others):
        if not paired:
            value = lax.all_to_all(value, "v", 0, 0, tiled=True)
            value = lax.all_to_all(value, "x", 1, 1, tiled=True)
            return value.transpose(0, 2, 1, 3, 4, 5)

        def take(row, column):
            return lax.dynamic_slice(value, (row, column, 0, 0, 0, 0), (1, 1) + value.shape[2:])[0]

        parts = (
            (take(v, x), v, x),
            (swap(take(v, 1 - x), "x"), v, 1 - x),
            (swap(take(1 - v, x), "v"), 1 - v, x),
            (lax.ppermute(take(1 - v, 1 - x), ("v", "x"), [(k, 3 - k) for k in range(4)]), 1 - v, 1 - x),
        )
        near, beside, above, across = (after(part, *others)[0] for part, _, _ in parts)
        mine = [jnp.where(x == 0, near, beside), jnp.where(x == 0, beside, near)]
        other = [jnp.where(x == 0, above, across), jnp.where(x == 0, across, above)]
        mine, other = jnp.stack(mine, axis=1), jnp.stack(other, axis=1)
        return jnp.stack([jnp.where(v == 0, mine, other), jnp.where(v == 0, other, mine)])

    results = []
    made, held = [], own
    for at in range(steps):
        chosen, base = (groups[-1:], sums[0]) if at < wide else (groups, None)
        made.append(contract(chosen, held, sib, flips, blocks, c, n_v, at, 1, n_orb, base))
        held = {o: after(array, made[-1]) for o, array in held.items()}
    for at, value in enumerate(made):
        value = exchange(value, *(made[at + 1 : at + 2] if at else ()))
        value = value.reshape((n_z, 2 * n_v // n_z) + value.shape[2:])
        value = after(value, *results[-1:])
        results.append(lax.all_to_all(value, "z", 0, 0, tiled=True))
    return finish(results)


def solution(mesh):
    n_ao, n_vir, n_occ = (mesh.shape[name] for name in ("ao", "vir", "occ"))
    fine = Mesh(mesh.devices.reshape(n_ao, n_vir // 2, 2, n_occ), ("z", "v", "c", "x"))
    vir = ("v", "c")
    return jax.shard_map(
        local,
        mesh=fine,
        in_specs=(P("x", None), P("z", "x", vir), P("z", None), P(vir, None), P(), P()),
        out_specs=P(vir, "x", "z"),
        check_vma=False,
    )
```
